32 devices in a mesh: groups: 2 (over x), corpus: 8 (over z, y), retrieve: 2 (over core).
Axes of the slice: x: 2, y: 2, z: 4, core: 2. Of those that a mesh axis runs over, the one named last changes fastest.
Arguments:
- weights: int32 [4], replicated, may hold values from 1 to 16
- q_wide: bfloat16 [2, 256, 4096], P('retrieve', ('groups', 'corpus')), parts along dimension 1
- q_mid: bfloat16 [256, 3584], P(('groups', 'corpus'), 'retrieve'), parts along dimension 0
- q_narrow: bfloat16 [256, 1024], P(('groups', 'corpus'), 'retrieve'), parts along dimension 0
- pass_wide: bfloat16 [2, 12288, 4096], P('retrieve', ('groups', 'corpus')), parts along dimension 1
- pass_mid: bfloat16 [12288, 3584], P(('groups', 'corpus'), 'retrieve'), parts along dimension 0
- pass_narrow: bfloat16 [12288, 1024], P(('groups', 'corpus'), 'retrieve'), parts along dimension 0
Outputs:
- united: float32 [128, 12288], P('retrieve', ('groups', 'corpus')), parts along dimension 1
The draws below stay inside these ranges and needn't reach their ends.
There are 2 independent parts, one for each index of `groups`. The reference program is written for one: setup_inputs(seed, part) draws one part's arguments, and reference() takes and returns one part's arrays. A program takes and returns all parts, laid end to end along the dimension named above; an argument that names none is the same for every part. Nothing has to cross between parts.
Inputs may be any that keep to these rules, and one draw needn't show every extreme that they name: `weights`: numerators over a fixed denominator of 16.
All inputs are finite; a program needn't handle non-finite values.
Results may differ from the reference program's by a relative error of at most 0.0003.
Values may be sent and summed in bfloat16 or wider, within the bound.
A program may use at most 128 MiB of HBM per device.

```python
import math
import jax
import jax.numpy as jnp
from jax import lax

WIDE = 4096
MID = 3584
NARROW = 1024
Q = 128
SLAB = 6144


def draw_q_wide(key, part):
    base_key = jax.random.fold_in(key, 11)
    table = jax.random.normal(base_key, (2, Q, WIDE), jnp.float32)
    return table.astype(jnp.bfloat16)


def draw_q_mid(key, part):
    base_key = jax.random.fold_in(key, 12)
    table = jax.random.normal(base_key, (Q, MID), jnp.float32)
    return table.astype(jnp.bfloat16)


def draw_q_narrow(key, part):
    base_key = jax.random.fold_in(key, 13)
    table = jax.random.normal(base_key, (Q, NARROW), jnp.float32)
    return table.astype(jnp.bfloat16)


def draw_pass_wide(key, part):
    base_key = jax.random.fold_in(key, 21)
    table = jax.random.normal(base_key, (2, SLAB, WIDE), jnp.float32)
    return table.astype(jnp.bfloat16)


def draw_pass_mid(key, part):
    base_key = jax.random.fold_in(key, 22)
    table = jax.random.normal(base_key, (SLAB, MID), jnp.float32)
    return table.astype(jnp.bfloat16)


def draw_pass_narrow(key, part):
    base_key = jax.random.fold_in(key, 23)
    table = jax.random.normal(base_key, (SLAB, NARROW), jnp.float32)
    return table.astype(jnp.bfloat16)


def place_ends(entries, key, least, top_value):
    longest = entries.shape.index(max(entries.shape))
    spots = []
    for shift in (0, 1):
        where = [jax.random.randint(jax.random.fold_in(key, axis), (), 0, length) for axis, length in enumerate(entries.shape)]
        where[longest] = (where[longest] + shift) % entries.shape[longest]
        spots.append(tuple(where))
    return entries.at[spots[0]].set(least).at[spots[1]].set(top_value)


def setup_inputs(seed: int = 0, part: int = 0) -> dict:
    streams_of = jax.random.split(jax.random.key(seed), 8)
    own_keys = jax.random.split(jax.random.fold_in(streams_of[7], part), 8)
    weights = place_ends(jax.random.randint(streams_of[0], (4,), 1, 17), jax.random.fold_in(streams_of[0], 1), 1, 16).astype(jnp.int32)
    q_wide = draw_q_wide(jax.random.fold_in(jax.random.fold_in(streams_of[7], part), 71), part)
    q_mid = draw_q_mid(jax.random.fold_in(jax.random.fold_in(streams_of[7], part), 71), part)
    q_narrow = draw_q_narrow(jax.random.fold_in(jax.random.fold_in(streams_of[7], part), 71), part)
    pass_wide = draw_pass_wide(jax.random.fold_in(jax.random.fold_in(streams_of[7], part), 71), part)
    pass_mid = draw_pass_mid(jax.random.fold_in(jax.random.fold_in(streams_of[7], part), 71), part)
    pass_narrow = draw_pass_narrow(jax.random.fold_in(jax.random.fold_in(streams_of[7], part), 71), part)
    return {"weights": weights, "q_wide": q_wide, "q_mid": q_mid, "q_narrow": q_narrow, "pass_wide": pass_wide, "pass_mid": pass_mid, "pass_narrow": pass_narrow}


unite_scale = 1.0 / 16.0

def label_probs(queries, passages, width):
    score = jnp.dot(queries, passages.T, preferred_element_type=jnp.float32) * (1.0 / math.sqrt(width))
    peak_rows = lax.optimization_barrier(jnp.max(score, axis=1, keepdims=True))
    powers = jnp.exp(score - peak_rows)
    totals = lax.optimization_barrier(jnp.sum(powers, axis=1, keepdims=True))
    return powers * (float(SLAB) / totals)

def reference(weights, q_wide, q_mid, q_narrow, pass_wide, pass_mid, pass_narrow):
    uniting = weights.astype(jnp.float32) * unite_scale
    united = uniting[0] * label_probs(q_wide[0], pass_wide[0], WIDE)
    united = united + uniting[1] * label_probs(q_wide[1], pass_wide[1], WIDE)
    united = united + uniting[2] * label_probs(q_mid, pass_mid, MID)
    united = united + uniting[3] * label_probs(q_narrow, pass_narrow, NARROW)
    return united
```

```python
import functools
import math

import jax
import jax.numpy as jnp
from jax import lax
from jax.experimental import pallas as pl
from jax.experimental.pallas import tpu as pltpu
from jax.sharding import PartitionSpec as P

WIDE = 4096
MID = 3584
NARROW = 1024
MESH = pl.DeviceIdType.MESH
LANES = 128
HALF = 64
TILE = 256


def pieces(narrow_cols, mid_cols, wide_cols):
    plan = []
    for which, cols, size in ((2, narrow_cols, 512), (1, mid_cols, 1024), (0, wide_cols, 1024)):
        at = 0
        while at < cols:
            step = min(size, cols - at)
            plan.append((which, at, step))
            at += step
    return plan


def each(count, step):
    if count <= 4:
        for i in range(count):
            step(i)
    else:
        lax.fori_loop(0, count, lambda i, _: (step(i), 0)[1], 0)


def kernel(
    nz, ny, plan,
    w_ref, qw, qm, qn, pw, pm, pn,
    out_ref,
    gw, gm, gn, vw, vm, vn, wide, part, got, tile, mixed, wide_stat, wide_all, mn_all,
    load_sem, pass_sem, send_sem, recv_sem, cross_sem, stat_sem,
):
    nc = nz * ny
    me = lax.axis_index("corpus")
    core = lax.axis_index("retrieve")
    other = 1 - core
    z, y = me // ny, me % ny
    rows = qw.shape[1]
    nq = rows * nc
    half = nq // 2
    nb = half // HALF
    slab = float(pw.shape[1] * nc)
    cols = pw.shape[1]
    own = (qw.at[0], qm, qn)
    full = (gw, gm, gn)
    held = (vw, vm, vn)
    source = (pw.at[0], pm, pn)

    barrier = pltpu.get_barrier_semaphore()

    def greet(j):
        s = lax.rem(me + j + 1, nc)
        for c in range(2):
            pl.semaphore_signal(
                barrier, inc=1, device_id={"corpus": s, "retrieve": c}, device_id_type=MESH
            )

    pl.semaphore_signal(barrier, inc=1, device_id={"retrieve": other}, device_id_type=MESH)
    each(nc - 1, greet)

    def load(i):
        return pltpu.make_async_copy(
            own[i], full[i].at[pl.ds(pl.multiple_of(me * rows, rows), rows)], load_sem.at[i]
        )

    def load_pass(k):
        which, at, step = plan[k]
        return pltpu.make_async_copy(
            source[which].at[:, pl.ds(at, step)],
            held[which].at[:, pl.ds(at, step)],
            pass_sem.at[k],
        )

    for i in range(3):
        load(i).start()
    for k in range(len(plan)):
        load_pass(k).start()

    pl.semaphore_wait(barrier, 2 * nc - 1)

    def block(k, s):
        which, at, step = plan[k]
        return full[which].at[pl.ds(pl.multiple_of(s * rows, rows), rows), pl.ds(at, step)]

    def push(k, s, to, src=None):
        which, at, step = plan[k]
        return pltpu.make_async_remote_copy(
            src_ref=block(k, s) if src is None else src,
            dst_ref=block(k, s),
            send_sem=send_sem.at[which],
            recv_sem=recv_sem.at[k, s],
            device_id={"corpus": to},
            device_id_type=MESH,
        )

    def first(k):
        which, at, step = plan[k]
        mine = own[which].at[:, pl.ds(at, step)]

        def along_y(j):
            push(k, me, z * ny + lax.rem(y + j + 1, ny), mine).start()

        def along_z(j):
            push(k, me, lax.rem(z + j + 1, nz) * ny + y, mine).start()

        each(nz - 1, along_z)
        each(ny - 1, along_y)

    for k in range(len(plan)):
        first(k)
    for i in range(3):
        load(i).wait()

    def forward(k):
        def arrived(j):
            s = lax.rem(z + j + 1, nz) * ny + y
            push(k, s, me).wait_recv()

            def on(i):
                push(k, s, z * ny + lax.rem(y + i + 1, ny)).start()

            each(ny - 1, on)

        each(nz - 1, arrived)

    def collect(k):
        def column(i):
            def row(j):
                s = lax.rem(z + j, nz) * ny + lax.rem(y + i + 1, ny)
                push(k, s, me).wait_recv()

            each(nz, row)

        each(ny - 1, column)

    def multiply(k):
        which, at, step = plan[k]
        load_pass(k).wait()
        into = (wide, part.at[0], part.at[1])[which]

        def product(t, r):
            n0 = pl.ds(pl.multiple_of(t * TILE, TILE), TILE)
            r0 = pl.ds(pl.multiple_of(r * LANES, LANES), LANES)
            value = lax.dot_general(
                full[which][r0, pl.ds(at, step)],
                held[which][n0, pl.ds(at, step)],
                (((1,), (1,)), ((), ())),
                preferred_element_type=jnp.float32,
            )
            if at == 0:
                into[r0, n0] = value
            else:
                into[r0, n0] += value

        each(nq // LANES, lambda r: each(cols // TILE, lambda t: product(t, r)))

    def cross(src, dst, i):
        return pltpu.make_async_remote_copy(
            src_ref=src,
            dst_ref=dst,
            send_sem=cross_sem.at[0, i],
            recv_sem=cross_sem.at[1, i],
            device_id={"retrieve": other},
            device_id_type=MESH,
        )

    def their_rows():
        return pl.ds(pl.multiple_of(other * half, half), half)

    def cross_part(i):
        return cross(part.at[i, their_rows()], got.at[i], i)

    def cross_tile():
        return cross(wide.at[their_rows()], tile, 2)

    def packed(peak, total):
        column = jnp.concatenate([peak, total], axis=0)
        return jnp.broadcast_to(column, (LANES, LANES)).T[0:1]

    def powers(score):
        peak = jnp.max(score, axis=1, keepdims=True)
        power = jnp.exp(score - peak)
        return power, packed(peak, jnp.sum(power, axis=1, keepdims=True))

    def factors(stats, mine, weight):
        top = jnp.max(stats, axis=0)
        grown = jnp.exp(stats - top[None])
        totals = jnp.stack([pltpu.roll(stats[s], HALF, 1) for s in range(stats.shape[0])])
        total = jnp.sum(grown * totals, axis=0)
        factor = jnp.exp(mine - top) * (slab / total) * weight
        return jnp.broadcast_to(factor, (LANES, LANES)).T[:HALF]

    def scaled(power, factor):
        return power * jnp.concatenate([factor] * (cols // LANES), axis=1)

    uniting = [w_ref[i].astype(jnp.float32) * (1.0 / 16.0) for i in range(4)]

    def mn_copy(to):
        return pltpu.make_async_remote_copy(
            src_ref=mn_all.at[me],
            dst_ref=mn_all.at[me],
            send_sem=stat_sem.at[0],
            recv_sem=stat_sem.at[1],
            device_id={"corpus": to},
            device_id_type=MESH,
        )

    def middle_stats():
        for i, width in ((0, MID), (1, NARROW)):
            cross_part(i).wait()
            for b in range(nb):
                rb = pl.ds(pl.multiple_of(core * half + b * HALF, HALF), HALF)
                gb = pl.ds(b * HALF, HALF)
                power, stat = powers((part[i, rb] + got[i, gb]) * (1.0 / math.sqrt(width)))
                got[i, gb] = power
                mn_all[me, i * nb + b] = stat
        each(nc - 1, lambda j: mn_copy(lax.rem(me + j + 1, nc)).start())

    def middle_mix():
        pltpu.make_async_remote_copy(
            src_ref=mn_all.at[pl.ds(0, nc - 1)],
            dst_ref=mn_all.at[pl.ds(0, nc - 1)],
            send_sem=stat_sem.at[0],
            recv_sem=stat_sem.at[1],
            device_id={"corpus": me},
            device_id_type=MESH,
        ).wait()
        for b in range(nb):
            gb = pl.ds(b * HALF, HALF)
            total = None
            for i in range(2):
                at = i * nb + b
                factor = factors(mn_all[:, at], mn_all[me, at], uniting[2 + i])
                term = scaled(got[i, gb], factor)
                total = term if total is None else total + term
            mixed[gb] = total

    def wide_copy(s, c):
        return pltpu.make_async_remote_copy(
            src_ref=wide_stat.at[c],
            dst_ref=wide_all.at[core * nc + me],
            send_sem=stat_sem.at[2],
            recv_sem=stat_sem.at[3],
            device_id={"corpus": s, "retrieve": c},
            device_id_type=MESH,
        )

    def wide_stats():
        for h in range(2):
            for b in range(nb):
                rb = pl.ds(h * half + b * HALF, HALF)
                power, stat = powers(wide[rb] * (1.0 / math.sqrt(WIDE)))
                wide[rb] = power
                wide_stat[h, b] = stat
        wide_all[core * nc + me] = wide_stat[core]

        def tell(j):
            s = lax.rem(me + j + 1, nc)
            for c in range(2):
                wide_copy(s, c).start()

        each(nc - 1, tell)
        wide_copy(me, other).start()
        cross_tile().start()

    def wide_mix():
        pltpu.make_async_remote_copy(
            src_ref=wide_all.at[pl.ds(0, 2 * nc - 1)],
            dst_ref=wide_all.at[pl.ds(0, 2 * nc - 1)],
            send_sem=stat_sem.at[2],
            recv_sem=stat_sem.at[3],
            device_id={"corpus": me},
            device_id_type=MESH,
        ).wait()
        here = [jnp.where(core == 0, uniting[0], uniting[1]), jnp.where(core == 0, uniting[1], uniting[0])]
        spans = []
        for b in range(nb):
            gb = pl.ds(b * HALF, HALF)
            rb = pl.ds(pl.multiple_of(core * half + b * HALF, HALF), HALF)
            mine = factors(wide_all[pl.ds(core * nc, nc), b], wide_all[core * nc + me, b], here[0])
            theirs = factors(wide_all[pl.ds(other * nc, nc), b], wide_all[other * nc + me, b], here[1])
            mixed[gb] += scaled(wide[rb], mine)
            spans.append((gb, theirs))
        cross_tile().wait()
        for gb, theirs in spans:
            out_ref[gb] = mixed[gb] + scaled(tile[gb], theirs)

    last = len(plan) - 1
    narrow_end = max(k for k in range(len(plan)) if plan[k][0] == 2)
    mid_end = max(k for k in range(len(plan)) if plan[k][0] == 1)
    forward(0)
    for k in range(len(plan)):
        if k < last:
            forward(k + 1)
        collect(k)
        multiply(k)
        if k == narrow_end:
            cross_part(1).start()
        if k == mid_end:
            cross_part(0).start()
        if k == mid_end + 1:
            middle_stats()
        if k == last - 1:
            middle_mix()
    wide_stats()
    wide_mix()
    for i in range(3):
        sent = full[i].at[pl.ds(0, (nc - 1) * rows)]
        pltpu.make_async_remote_copy(
            src_ref=sent,
            dst_ref=sent,
            send_sem=send_sem.at[i],
            recv_sem=recv_sem.at[0, 0],
            device_id={"corpus": me},
            device_id_type=MESH,
        ).wait_send()


def body(weights, q_wide, q_mid, q_narrow, pass_wide, pass_mid, pass_narrow):
    nc = lax.axis_size("corpus")
    ny = 1
    while 4 * ny * ny <= nc:
        ny *= 2
    nz = nc // ny
    nq = q_wide.shape[1] * nc
    half = nq // 2
    nb = half // HALF
    cols = pass_wide.shape[1]
    wide_cols, mid_cols, narrow_cols = q_wide.shape[2], q_mid.shape[1], q_narrow.shape[1]
    plan = pieces(narrow_cols, mid_cols, wide_cols)
    f32, bf16 = jnp.float32, jnp.bfloat16
    hbm = pl.BlockSpec(memory_space=pl.ANY)
    features = wide_cols + mid_cols + narrow_cols
    return pl.pallas_call(
        functools.partial(kernel, nz, ny, plan),
        out_shape=jax.ShapeDtypeStruct((half, cols), f32),
        in_specs=[pl.BlockSpec(memory_space=pltpu.SMEM)] + [hbm] * 6,
        out_specs=pl.BlockSpec(memory_space=pltpu.VMEM),
        scratch_shapes=[
            pltpu.VMEM((nq, wide_cols), bf16),
            pltpu.VMEM((nq, mid_cols), bf16),
            pltpu.VMEM((nq, narrow_cols), bf16),
            pltpu.VMEM((cols, wide_cols), bf16),
            pltpu.VMEM((cols, mid_cols), bf16),
            pltpu.VMEM((cols, narrow_cols), bf16),
            pltpu.VMEM((nq, cols), f32),
            pltpu.VMEM((2, nq, cols), f32),
            pltpu.VMEM((2, half, cols), f32),
            pltpu.VMEM((half, cols), f32),
            pltpu.VMEM((half, cols), f32),
            pltpu.VMEM((2, nb, 1, LANES), f32),
            pltpu.VMEM((2 * nc, nb, 1, LANES), f32),
            pltpu.VMEM((nc, 2 * nb, 1, LANES), f32),
            pltpu.SemaphoreType.DMA((3,)),
            pltpu.SemaphoreType.DMA((len(plan),)),
            pltpu.SemaphoreType.DMA((3,)),
            pltpu.SemaphoreType.DMA((len(plan), nc)),
            pltpu.SemaphoreType.DMA((2, 3)),
            pltpu.SemaphoreType.DMA((4,)),
        ],
        compiler_params=pltpu.CompilerParams(
            collective_id=0, has_side_effects=True, vmem_limit_bytes=60 * 1024 * 1024
        ),
        cost_estimate=pl.CostEstimate(
            flops=2 * nq * cols * features,
            bytes_accessed=2 * cols * features,
            transcendentals=2 * nq * cols,
        ),
    )(weights, q_wide, q_mid, q_narrow, pass_wide, pass_mid, pass_narrow)


def solution(mesh):
    return jax.shard_map(
        body,
        mesh=mesh,
        in_specs=(
            P(),
            P("retrieve", ("groups", "corpus"), None),
            P(("groups", "corpus"), "retrieve"),
            P(("groups", "corpus"), "retrieve"),
            P("retrieve", ("groups", "corpus"), None),
            P(("groups", "corpus"), "retrieve"),
            P(("groups", "corpus"), "retrieve"),
        ),
        out_specs=P("retrieve", ("groups", "corpus")),
        check_vma=False,
    )
```

```python
import functools
import math

import jax
import jax.numpy as jnp
from jax import lax
from jax.experimental import pallas as pl
from jax.experimental.pallas import tpu as pltpu
from jax.sharding import PartitionSpec as P

WIDE = 4096
MID = 3584
NARROW = 1024
MESH = pl.DeviceIdType.MESH
LANES = 128
HALF = 64
TILE = 256


def pieces(narrow_cols, mid_cols, wide_cols):
    plan = []
    for which, cols, size in ((2, narrow_cols, 512), (1, mid_cols, 1024), (0, wide_cols, 1024)):
        at = 0
        while at < cols:
            step = min(size, cols - at)
            plan.append((which, at, step))
            at += step
    return plan


def each(count, step):
    if count <= 4:
        for i in range(count):
            step(i)
    else:
        lax.fori_loop(0, count, lambda i, _: (step(i), 0)[1], 0)


def kernel(
    nz, ny, plan,
    w_ref, qw, qm, qn, pw, pm, pn,
    out_ref,
    gw, gm, gn, vw, vm, vn, wide, part, got, tile, mixed, wide_stat, wide_all, mn_all,
    load_sem, pass_sem, send_sem, recv_sem, cross_sem, stat_sem,
):
    nc = nz * ny
    me = lax.axis_index("corpus")
    core = lax.axis_index("retrieve")
    other = 1 - core
    z, y = me // ny, me % ny
    rows = qw.shape[1]
    nq = rows * nc
    half = nq // 2
    nb = half // HALF
    slab = float(pw.shape[1] * nc)
    cols = pw.shape[1]
    own = (qw.at[0], qm, qn)
    full = (gw, gm, gn)
    held = (vw, vm, vn)
    source = (pw.at[0], pm, pn)

    barrier = pltpu.get_barrier_semaphore()

    up, down = z + 1 < nz, z > 0
    neighbours = 1 + (ny - 1) + up.astype(jnp.int32) + down.astype(jnp.int32)

    def greet(s):
        pl.semaphore_signal(barrier, inc=1, device_id={"corpus": s}, device_id_type=MESH)

    pl.semaphore_signal(barrier, inc=1, device_id={"retrieve": other}, device_id_type=MESH)
    each(ny - 1, lambda j: greet(z * ny + lax.rem(y + j + 1, ny)))
    pl.when(up)(lambda: greet(me + ny))
    pl.when(down)(lambda: greet(me - ny))

    def load(i):
        return pltpu.make_async_copy(
            own[i], full[i].at[pl.ds(pl.multiple_of(me * rows, rows), rows)], load_sem.at[i]
        )

    def load_pass(k):
        which, at, step = plan[k]
        return pltpu.make_async_copy(
            source[which].at[:, pl.ds(at, step)],
            held[which].at[:, pl.ds(at, step)],
            pass_sem.at[k],
        )

    for i in range(3):
        load(i).start()
    for k in range(len(plan)):
        load_pass(k).start()

    pl.semaphore_wait(barrier, neighbours)

    def block(k, s):
        which, at, step = plan[k]
        return full[which].at[pl.ds(pl.multiple_of(s * rows, rows), rows), pl.ds(at, step)]

    def push(k, s, to, way, src=None):
        which, at, step = plan[k]
        return pltpu.make_async_remote_copy(
            src_ref=block(k, s) if src is None else src,
            dst_ref=block(k, s),
            send_sem=send_sem.at[way, which],
            recv_sem=recv_sem.at[k, s],
            device_id={"corpus": to},
            device_id_type=MESH,
        )

    def first(k):
        which, at, step = plan[k]
        mine = own[which].at[:, pl.ds(at, step)]

        pl.when(up)(lambda: push(k, me, me + ny, 0, mine).start())
        pl.when(down)(lambda: push(k, me, me - ny, 1, mine).start())
        each(ny - 1, lambda j: push(k, me, z * ny + lax.rem(y + j + 1, ny), 2, mine).start())

    for i in range(3):
        load(i).wait()

    def relay(k, t):
        def arrived(s, more, ahead, way):
            push(k, s, me, way).wait_recv()
            pl.when(more)(lambda: push(k, s, ahead, way).start())
            each(ny - 1, lambda j: push(k, s, z * ny + lax.rem(y + j + 1, ny), 2).start())

        pl.when(z >= t)(lambda: arrived(me - t * ny, up, me + ny, 0))
        pl.when(z + t < nz)(lambda: arrived(me + t * ny, down, me - ny, 1))

    def collect(k):
        def column(i):
            def row(j):
                s = lax.rem(z + j, nz) * ny + lax.rem(y + i + 1, ny)
                push(k, s, me, 2).wait_recv()

            each(nz, row)

        each(ny - 1, column)

    def multiply(k):
        which, at, step = plan[k]
        load_pass(k).wait()
        into = (wide, part.at[0], part.at[1])[which]

        def product(t, r):
            n0 = pl.ds(pl.multiple_of(t * TILE, TILE), TILE)
            r0 = pl.ds(pl.multiple_of(r * LANES, LANES), LANES)
            value = lax.dot_general(
                full[which][r0, pl.ds(at, step)],
                held[which][n0, pl.ds(at, step)],
                (((1,), (1,)), ((), ())),
                preferred_element_type=jnp.float32,
            )
            if at == 0:
                into[r0, n0] = value
            else:
                into[r0, n0] += value

        each(nq // LANES, lambda r: each(cols // TILE, lambda t: product(t, r)))

    def cross(src, dst, i):
        return pltpu.make_async_remote_copy(
            src_ref=src,
            dst_ref=dst,
            send_sem=cross_sem.at[0, i],
            recv_sem=cross_sem.at[1, i],
            device_id={"retrieve": other},
            device_id_type=MESH,
        )

    def their_rows():
        return pl.ds(pl.multiple_of(other * half, half), half)

    def cross_part(i):
        return cross(part.at[i, their_rows()], got.at[i], i)

    def cross_tile():
        return cross(wide.at[their_rows()], tile, 2)

    def packed(peak, total):
        column = jnp.concatenate([peak, total], axis=0)
        return jnp.broadcast_to(column, (LANES, LANES)).T[0:1]

    def powers(score):
        peak = jnp.max(score, axis=1, keepdims=True)
        power = jnp.exp(score - peak)
        return power, packed(peak, jnp.sum(power, axis=1, keepdims=True))

    def factors(stats, mine, weight):
        top = jnp.max(stats, axis=0)
        grown = jnp.exp(stats - top[None])
        totals = jnp.stack([pltpu.roll(stats[s], HALF, 1) for s in range(stats.shape[0])])
        total = jnp.sum(grown * totals, axis=0)
        factor = jnp.exp(mine - top) * (slab / total) * weight
        return jnp.broadcast_to(factor, (LANES, LANES)).T[:HALF]

    def scaled(power, factor):
        return power * jnp.concatenate([factor] * (cols // LANES), axis=1)

    uniting = [w_ref[i].astype(jnp.float32) * (1.0 / 16.0) for i in range(4)]

    def mn_copy(to):
        return pltpu.make_async_remote_copy(
            src_ref=mn_all.at[me],
            dst_ref=mn_all.at[me],
            send_sem=stat_sem.at[0],
            recv_sem=stat_sem.at[1],
            device_id={"corpus": to},
            device_id_type=MESH,
        )

    def middle_stats():
        for i, width in ((0, MID), (1, NARROW)):
            cross_part(i).wait()
            for b in range(nb):
                rb = pl.ds(pl.multiple_of(core * half + b * HALF, HALF), HALF)
                gb = pl.ds(b * HALF, HALF)
                power, stat = powers((part[i, rb] + got[i, gb]) * (1.0 / math.sqrt(width)))
                got[i, gb] = power
                mn_all[me, i * nb + b] = stat
        each(nc - 1, lambda j: mn_copy(lax.rem(me + j + 1, nc)).start())

    def middle_mix():
        pltpu.make_async_remote_copy(
            src_ref=mn_all.at[pl.ds(0, nc - 1)],
            dst_ref=mn_all.at[pl.ds(0, nc - 1)],
            send_sem=stat_sem.at[0],
            recv_sem=stat_sem.at[1],
            device_id={"corpus": me},
            device_id_type=MESH,
        ).wait()
        for b in range(nb):
            gb = pl.ds(b * HALF, HALF)
            total = None
            for i in range(2):
                at = i * nb + b
                factor = factors(mn_all[:, at], mn_all[me, at], uniting[2 + i])
                term = scaled(got[i, gb], factor)
                total = term if total is None else total + term
            mixed[gb] = total

    def wide_copy(s, c):
        return pltpu.make_async_remote_copy(
            src_ref=wide_stat.at[c],
            dst_ref=wide_all.at[core * nc + me],
            send_sem=stat_sem.at[2],
            recv_sem=stat_sem.at[3],
            device_id={"corpus": s, "retrieve": c},
            device_id_type=MESH,
        )

    def wide_stats():
        for h in range(2):
            for b in range(nb):
                rb = pl.ds(h * half + b * HALF, HALF)
                power, stat = powers(wide[rb] * (1.0 / math.sqrt(WIDE)))
                wide[rb] = power
                wide_stat[h, b] = stat
        wide_all[core * nc + me] = wide_stat[core]

        def tell(j):
            s = lax.rem(me + j + 1, nc)
            for c in range(2):
                wide_copy(s, c).start()

        each(nc - 1, tell)
        wide_copy(me, other).start()
        cross_tile().start()

    def wide_mix():
        pltpu.make_async_remote_copy(
            src_ref=wide_all.at[pl.ds(0, 2 * nc - 1)],
            dst_ref=wide_all.at[pl.ds(0, 2 * nc - 1)],
            send_sem=stat_sem.at[2],
            recv_sem=stat_sem.at[3],
            device_id={"corpus": me},
            device_id_type=MESH,
        ).wait()
        here = [jnp.where(core == 0, uniting[0], uniting[1]), jnp.where(core == 0, uniting[1], uniting[0])]
        spans = []
        for b in range(nb):
            gb = pl.ds(b * HALF, HALF)
            rb = pl.ds(pl.multiple_of(core * half + b * HALF, HALF), HALF)
            mine = factors(wide_all[pl.ds(core * nc, nc), b], wide_all[core * nc + me, b], here[0])
            theirs = factors(wide_all[pl.ds(other * nc, nc), b], wide_all[other * nc + me, b], here[1])
            mixed[gb] += scaled(wide[rb], mine)
            spans.append((gb, theirs))
        cross_tile().wait()
        for gb, theirs in spans:
            out_ref[gb] = mixed[gb] + scaled(tile[gb], theirs)

    narrow_end = max(k for k in range(len(plan)) if plan[k][0] == 2)
    mid_end = max(k for k in range(len(plan)) if plan[k][0] == 1)
    early = range(mid_end + 1)
    late = range(mid_end + 1, len(plan))
    cut = mid_end + 1 + len(late) // 2
    for k in range(cut):
        first(k)
    for k in early:
        relay(k, 1)
    for k in range(cut, len(plan)):
        first(k)
    for t in range(2, nz):
        for k in early:
            relay(k, t)
    for t in range(1, nz):
        for k in late:
            relay(k, t)
        if t == 1:
            for k in early:
                collect(k)
                multiply(k)
                if k == narrow_end:
                    cross_part(1).start()
            cross_part(0).start()
        if t == 2:
            middle_stats()
    for k in late:
        collect(k)
        multiply(k)
        if k == late[len(late) // 2]:
            middle_mix()
    wide_stats()
    wide_mix()

    def sent(way, i, count):
        some = full[i].at[pl.ds(0, count * rows)]
        pltpu.make_async_remote_copy(
            src_ref=some,
            dst_ref=some,
            send_sem=send_sem.at[way, i],
            recv_sem=recv_sem.at[0, 0],
            device_id={"corpus": me},
            device_id_type=MESH,
        ).wait_send()

    for i in range(3):
        for at in range(nz - 1):
            pl.when(z == at)(lambda i=i, at=at: sent(0, i, at + 1))
            pl.when(z == at + 1)(lambda i=i, at=at: sent(1, i, nz - at - 1))
        sent(2, i, nz * (ny - 1))


def body(weights, q_wide, q_mid, q_narrow, pass_wide, pass_mid, pass_narrow):
    nc = lax.axis_size("corpus")
    ny = 1
    while 4 * ny * ny <= nc:
        ny *= 2
    nz = nc // ny
    nq = q_wide.shape[1] * nc
    half = nq // 2
    nb = half // HALF
    cols = pass_wide.shape[1]
    wide_cols, mid_cols, narrow_cols = q_wide.shape[2], q_mid.shape[1], q_narrow.shape[1]
    plan = pieces(narrow_cols, mid_cols, wide_cols)
    f32, bf16 = jnp.float32, jnp.bfloat16
    hbm = pl.BlockSpec(memory_space=pl.ANY)
    features = wide_cols + mid_cols + narrow_cols
    return pl.pallas_call(
        functools.partial(kernel, nz, ny, plan),
        out_shape=jax.ShapeDtypeStruct((half, cols), f32),
        in_specs=[pl.BlockSpec(memory_space=pltpu.SMEM)] + [hbm] * 6,
        out_specs=pl.BlockSpec(memory_space=pltpu.VMEM),
        scratch_shapes=[
            pltpu.VMEM((nq, wide_cols), bf16),
            pltpu.VMEM((nq, mid_cols), bf16),
            pltpu.VMEM((nq, narrow_cols), bf16),
            pltpu.VMEM((cols, wide_cols), bf16),
            pltpu.VMEM((cols, mid_cols), bf16),
            pltpu.VMEM((cols, narrow_cols), bf16),
            pltpu.VMEM((nq, cols), f32),
            pltpu.VMEM((2, nq, cols), f32),
            pltpu.VMEM((2, half, cols), f32),
            pltpu.VMEM((half, cols), f32),
            pltpu.VMEM((half, cols), f32),
            pltpu.VMEM((2, nb, 1, LANES), f32),
            pltpu.VMEM((2 * nc, nb, 1, LANES), f32),
            pltpu.VMEM((nc, 2 * nb, 1, LANES), f32),
            pltpu.SemaphoreType.DMA((3,)),
            pltpu.SemaphoreType.DMA((len(plan),)),
            pltpu.SemaphoreType.DMA((3, 3)),
            pltpu.SemaphoreType.DMA((len(plan), nc)),
            pltpu.SemaphoreType.DMA((2, 3)),
            pltpu.SemaphoreType.DMA((4,)),
        ],
        compiler_params=pltpu.CompilerParams(
            collective_id=0, has_side_effects=True, vmem_limit_bytes=60 * 1024 * 1024
        ),
        cost_estimate=pl.CostEstimate(
            flops=2 * nq * cols * features,
            bytes_accessed=2 * cols * features,
            transcendentals=2 * nq * cols,
        ),
    )(weights, q_wide, q_mid, q_narrow, pass_wide, pass_mid, pass_narrow)


def solution(mesh):
    return jax.shard_map(
        body,
        mesh=mesh,
        in_specs=(
            P(),
            P("retrieve", ("groups", "corpus"), None),
            P(("groups", "corpus"), "retrieve"),
            P(("groups", "corpus"), "retrieve"),
            P("retrieve", ("groups", "corpus"), None),
            P(("groups", "corpus"), "retrieve"),
            P(("groups", "corpus"), "retrieve"),
        ),
        out_specs=P("retrieve", ("groups", "corpus")),
        check_vma=False,
    )
```

```python
import functools
import math

import jax
import jax.numpy as jnp
from jax import lax
from jax.experimental import pallas as pl
from jax.experimental.pallas import tpu as pltpu
from jax.sharding import PartitionSpec as P

WIDE = 4096
MID = 3584
NARROW = 1024
MESH = pl.DeviceIdType.MESH
LANES = 128
HALF = 64
TILE = 256


def pieces(narrow_cols, mid_cols, wide_cols):
    plan = []
    for which, cols, size in ((2, narrow_cols, 512), (1, mid_cols, 1024), (0, wide_cols, 1024)):
        at = 0
        while at < cols:
            step = min(size, cols - at)
            plan.append((which, at, step))
            at += step
    return plan


def each(count, step):
    if count <= 4:
        for i in range(count):
            step(i)
    else:
        lax.fori_loop(0, count, lambda i, _: (step(i), 0)[1], 0)


def kernel(
    nz, ny, plan,
    w_ref, qw, qm, qn, pw, pm, pn,
    out_ref,
    gw, gm, gn, vw, vm, vn, wide, part, got, tile, mixed, wide_stat, wide_all, mn_all,
    load_sem, pass_sem, send_sem, recv_sem, cross_sem, stat_sem,
):
    nc = nz * ny
    me = lax.axis_index("corpus")
    core = lax.axis_index("retrieve")
    other = 1 - core
    z, y = me // ny, me % ny
    rows = qw.shape[1]
    nq = rows * nc
    half = nq // 2
    nb = half // HALF
    slab = float(pw.shape[1] * nc)
    cols = pw.shape[1]
    own = (qw.at[0], qm, qn)
    full = (gw, gm, gn)
    held = (vw, vm, vn)
    source = (pw.at[0], pm, pn)

    barrier = pltpu.get_barrier_semaphore()

    up, down = z + 1 < nz, z > 0
    neighbours = 1 + (ny - 1) + up.astype(jnp.int32) + down.astype(jnp.int32)

    def greet(s):
        pl.semaphore_signal(barrier, inc=1, device_id={"corpus": s}, device_id_type=MESH)

    pl.semaphore_signal(barrier, inc=1, device_id={"retrieve": other}, device_id_type=MESH)
    each(ny - 1, lambda j: greet(z * ny + lax.rem(y + j + 1, ny)))
    pl.when(up)(lambda: greet(me + ny))
    pl.when(down)(lambda: greet(me - ny))

    def load(i):
        return pltpu.make_async_copy(
            own[i], full[i].at[pl.ds(pl.multiple_of(me * rows, rows), rows)], load_sem.at[i]
        )

    def load_pass(k):
        which, at, step = plan[k]
        return pltpu.make_async_copy(
            source[which].at[:, pl.ds(at, step)],
            held[which].at[:, pl.ds(at, step)],
            pass_sem.at[k],
        )

    for i in range(3):
        load(i).start()
    for k in range(sum(which > 0 for which, _, _ in plan)):
        load_pass(k).start()

    for i in range(3):
        load(i).wait()
    pl.semaphore_wait(barrier, neighbours)

    def block(k, s):
        which, at, step = plan[k]
        return full[which].at[pl.ds(pl.multiple_of(s * rows, rows), rows), pl.ds(at, step)]

    def push(k, s, to, way, src=None):
        which, at, step = plan[k]
        return pltpu.make_async_remote_copy(
            src_ref=block(k, s) if src is None else src,
            dst_ref=block(k, s),
            send_sem=send_sem.at[way, which],
            recv_sem=recv_sem.at[k, s],
            device_id={"corpus": to},
            device_id_type=MESH,
        )

    def first(k):
        which, at, step = plan[k]
        mine = None

        pl.when(up)(lambda: push(k, me, me + ny, 0, mine).start())
        pl.when(down)(lambda: push(k, me, me - ny, 1, mine).start())
        each(ny - 1, lambda j: push(k, me, z * ny + lax.rem(y + j + 1, ny), 2, mine).start())


    def relay(k, t):
        def arrived(s, more, ahead, way):
            push(k, s, me, way).wait_recv()
            pl.when(more)(lambda: push(k, s, ahead, way).start())
            each(ny - 1, lambda j: push(k, s, z * ny + lax.rem(y + j + 1, ny), 2).start())

        pl.when(z >= t)(lambda: arrived(me - t * ny, up, me + ny, 0))
        pl.when(z + t < nz)(lambda: arrived(me + t * ny, down, me - ny, 1))

    def collect(k):
        def column(i):
            def row(j):
                s = lax.rem(z + j, nz) * ny + lax.rem(y + i + 1, ny)
                push(k, s, me, 2).wait_recv()

            each(nz, row)

        each(ny - 1, column)

    def multiply(k):
        which, at, step = plan[k]
        load_pass(k).wait()
        into = (wide, part.at[0], part.at[1])[which]

        def product(t, r):
            n0 = pl.ds(pl.multiple_of(t * TILE, TILE), TILE)
            r0 = pl.ds(pl.multiple_of(r * LANES, LANES), LANES)
            value = lax.dot_general(
                full[which][r0, pl.ds(at, step)],
                held[which][n0, pl.ds(at, step)],
                (((1,), (1,)), ((), ())),
                preferred_element_type=jnp.float32,
            )
            if at == 0:
                into[r0, n0] = value
            else:
                into[r0, n0] += value

        each(nq // LANES, lambda r: each(cols // TILE, lambda t: product(t, r)))

    def cross(src, dst, i):
        return pltpu.make_async_remote_copy(
            src_ref=src,
            dst_ref=dst,
            send_sem=cross_sem.at[0, i],
            recv_sem=cross_sem.at[1, i],
            device_id={"retrieve": other},
            device_id_type=MESH,
        )

    def their_rows():
        return pl.ds(pl.multiple_of(other * half, half), half)

    def cross_part(i):
        return cross(part.at[i, their_rows()], got.at[i], i)

    def cross_tile():
        return cross(wide.at[their_rows()], tile, 2)

    def packed(peak, total):
        column = jnp.concatenate([peak, total], axis=0)
        return jnp.broadcast_to(column, (LANES, LANES)).T[0:1]

    def powers(score):
        peak = jnp.max(score, axis=1, keepdims=True)
        power = jnp.exp(score - peak)
        return power, packed(peak, jnp.sum(power, axis=1, keepdims=True))

    def factors(stats, mine, weight):
        top = jnp.max(stats, axis=0)
        grown = jnp.exp(stats - top[None])
        totals = jnp.stack([pltpu.roll(stats[s], HALF, 1) for s in range(stats.shape[0])])
        total = jnp.sum(grown * totals, axis=0)
        factor = jnp.exp(mine - top) * (slab / total) * weight
        return jnp.broadcast_to(factor, (LANES, LANES)).T[:HALF]

    def scaled(power, factor):
        return power * jnp.concatenate([factor] * (cols // LANES), axis=1)

    uniting = [w_ref[i].astype(jnp.float32) * (1.0 / 16.0) for i in range(4)]

    def mn_copy(to):
        return pltpu.make_async_remote_copy(
            src_ref=mn_all.at[me],
            dst_ref=mn_all.at[me],
            send_sem=stat_sem.at[0],
            recv_sem=stat_sem.at[1],
            device_id={"corpus": to},
            device_id_type=MESH,
        )

    def middle_stats():
        for i, width in ((0, MID), (1, NARROW)):
            cross_part(i).wait()
            for b in range(nb):
                rb = pl.ds(pl.multiple_of(core * half + b * HALF, HALF), HALF)
                gb = pl.ds(b * HALF, HALF)
                power, stat = powers((part[i, rb] + got[i, gb]) * (1.0 / math.sqrt(width)))
                got[i, gb] = power
                mn_all[me, i * nb + b] = stat
        each(nc - 1, lambda j: mn_copy(lax.rem(me + j + 1, nc)).start())

    def middle_mix():
        pltpu.make_async_remote_copy(
            src_ref=mn_all.at[pl.ds(0, nc - 1)],
            dst_ref=mn_all.at[pl.ds(0, nc - 1)],
            send_sem=stat_sem.at[0],
            recv_sem=stat_sem.at[1],
            device_id={"corpus": me},
            device_id_type=MESH,
        ).wait()
        for b in range(nb):
            gb = pl.ds(b * HALF, HALF)
            total = None
            for i in range(2):
                at = i * nb + b
                factor = factors(mn_all[:, at], mn_all[me, at], uniting[2 + i])
                term = scaled(got[i, gb], factor)
                total = term if total is None else total + term
            mixed[gb] = total

    def wide_copy(s, c):
        return pltpu.make_async_remote_copy(
            src_ref=wide_stat.at[c],
            dst_ref=wide_all.at[core * nc + me],
            send_sem=stat_sem.at[2],
            recv_sem=stat_sem.at[3],
            device_id={"corpus": s, "retrieve": c},
            device_id_type=MESH,
        )

    def wide_stats():
        for h in range(2):
            for b in range(nb):
                rb = pl.ds(h * half + b * HALF, HALF)
                power, stat = powers(wide[rb] * (1.0 / math.sqrt(WIDE)))
                wide[rb] = power
                wide_stat[h, b] = stat
        wide_all[core * nc + me] = wide_stat[core]

        def tell(j):
            s = lax.rem(me + j + 1, nc)
            for c in range(2):
                wide_copy(s, c).start()

        each(nc - 1, tell)
        wide_copy(me, other).start()
        cross_tile().start()

    def wide_mix():
        pltpu.make_async_remote_copy(
            src_ref=wide_all.at[pl.ds(0, 2 * nc - 1)],
            dst_ref=wide_all.at[pl.ds(0, 2 * nc - 1)],
            send_sem=stat_sem.at[2],
            recv_sem=stat_sem.at[3],
            device_id={"corpus": me},
            device_id_type=MESH,
        ).wait()
        here = [jnp.where(core == 0, uniting[0], uniting[1]), jnp.where(core == 0, uniting[1], uniting[0])]
        spans = []
        for b in range(nb):
            gb = pl.ds(b * HALF, HALF)
            rb = pl.ds(pl.multiple_of(core * half + b * HALF, HALF), HALF)
            mine = factors(wide_all[pl.ds(core * nc, nc), b], wide_all[core * nc + me, b], here[0])
            theirs = factors(wide_all[pl.ds(other * nc, nc), b], wide_all[other * nc + me, b], here[1])
            mixed[gb] += scaled(wide[rb], mine)
            spans.append((gb, theirs))
        cross_tile().wait()
        for gb, theirs in spans:
            out_ref[gb] = mixed[gb] + scaled(tile[gb], theirs)

    narrow_end = max(k for k in range(len(plan)) if plan[k][0] == 2)
    mid_end = max(k for k in range(len(plan)) if plan[k][0] == 1)
    early = range(mid_end + 1)
    late = range(mid_end + 1, len(plan))
    cut = mid_end + 1 + len(late) // 2
    for k in range(cut):
        first(k)
    for k in early:
        relay(k, 1)
    for k in range(cut, len(plan)):
        first(k)
    for t in range(2, nz):
        for k in early:
            relay(k, t)
    for t in range(1, nz):
        for k in late:
            relay(k, t)
            if t == 1:
                load_pass(k).start()
        if t == 1:
            for k in early:
                collect(k)
                multiply(k)
                if k == narrow_end:
                    cross_part(1).start()
            cross_part(0).start()
        if t == 2:
            middle_stats()
    for k in late:
        collect(k)
        multiply(k)
        if k == late[len(late) // 2]:
            middle_mix()
    wide_stats()
    wide_mix()

    def sent(way, i, count):
        some = full[i].at[pl.ds(0, count * rows)]
        pltpu.make_async_remote_copy(
            src_ref=some,
            dst_ref=some,
            send_sem=send_sem.at[way, i],
            recv_sem=recv_sem.at[0, 0],
            device_id={"corpus": me},
            device_id_type=MESH,
        ).wait_send()

    for i in range(3):
        for at in range(nz - 1):
            pl.when(z == at)(lambda i=i, at=at: sent(0, i, at + 1))
            pl.when(z == at + 1)(lambda i=i, at=at: sent(1, i, nz - at - 1))
        sent(2, i, nz * (ny - 1))


def body(weights, q_wide, q_mid, q_narrow, pass_wide, pass_mid, pass_narrow):
    nc = lax.axis_size("corpus")
    ny = 1
    while 4 * ny * ny <= nc:
        ny *= 2
    nz = nc // ny
    nq = q_wide.shape[1] * nc
    half = nq // 2
    nb = half // HALF
    cols = pass_wide.shape[1]
    wide_cols, mid_cols, narrow_cols = q_wide.shape[2], q_mid.shape[1], q_narrow.shape[1]
    plan = pieces(narrow_cols, mid_cols, wide_cols)
    f32, bf16 = jnp.float32, jnp.bfloat16
    hbm = pl.BlockSpec(memory_space=pl.ANY)
    features = wide_cols + mid_cols + narrow_cols
    return pl.pallas_call(
        functools.partial(kernel, nz, ny, plan),
        out_shape=jax.ShapeDtypeStruct((half, cols), f32),
        in_specs=[pl.BlockSpec(memory_space=pltpu.SMEM)] + [hbm] * 6,
        out_specs=pl.BlockSpec(memory_space=pltpu.VMEM),
        scratch_shapes=[
            pltpu.VMEM((nq, wide_cols), bf16),
            pltpu.VMEM((nq, mid_cols), bf16),
            pltpu.VMEM((nq, narrow_cols), bf16),
            pltpu.VMEM((cols, wide_cols), bf16),
            pltpu.VMEM((cols, mid_cols), bf16),
            pltpu.VMEM((cols, narrow_cols), bf16),
            pltpu.VMEM((nq, cols), f32),
            pltpu.VMEM((2, nq, cols), f32),
            pltpu.VMEM((2, half, cols), f32),
            pltpu.VMEM((half, cols), f32),
            pltpu.VMEM((half, cols), f32),
            pltpu.VMEM((2, nb, 1, LANES), f32),
            pltpu.VMEM((2 * nc, nb, 1, LANES), f32),
            pltpu.VMEM((nc, 2 * nb, 1, LANES), f32),
            pltpu.SemaphoreType.DMA((3,)),
            pltpu.SemaphoreType.DMA((len(plan),)),
            pltpu.SemaphoreType.DMA((3, 3)),
            pltpu.SemaphoreType.DMA((len(plan), nc)),
            pltpu.SemaphoreType.DMA((2, 3)),
            pltpu.SemaphoreType.DMA((4,)),
        ],
        compiler_params=pltpu.CompilerParams(
            collective_id=0, has_side_effects=True, vmem_limit_bytes=60 * 1024 * 1024
        ),
        cost_estimate=pl.CostEstimate(
            flops=2 * nq * cols * features,
            bytes_accessed=2 * cols * features,
            transcendentals=2 * nq * cols,
        ),
    )(weights, q_wide, q_mid, q_narrow, pass_wide, pass_mid, pass_narrow)


def solution(mesh):
    return jax.shard_map(
        body,
        mesh=mesh,
        in_specs=(
            P(),
            P("retrieve", ("groups", "corpus"), None),
            P(("groups", "corpus"), "retrieve"),
            P(("groups", "corpus"), "retrieve"),
            P("retrieve", ("groups", "corpus"), None),
            P(("groups", "corpus"), "retrieve"),
            P(("groups", "corpus"), "retrieve"),
        ),
        out_specs=P("retrieve", ("groups", "corpus")),
        check_vma=False,
    )
```

```python
import functools
import math

import jax
import jax.numpy as jnp
from jax import lax
from jax.experimental import pallas as pl
from jax.experimental.pallas import tpu as pltpu
from jax.sharding import PartitionSpec as P

WIDE = 4096
MID = 3584
NARROW = 1024
MESH = pl.DeviceIdType.MESH
LANES = 128
HALF = 64
TILE = 256


def pieces(narrow_cols, mid_cols, wide_cols):
    plan = []
    for which, cols, size in ((2, narrow_cols, 512), (1, mid_cols, 1024), (0, wide_cols, 1024)):
        at = 0
        while at < cols:
            step = min(size, cols - at)
            plan.append((which, at, step))
            at += step
    return plan


def each(count, step):
    if count <= 4:
        for i in range(count):
            step(i)
    else:
        lax.fori_loop(0, count, lambda i, _: (step(i), 0)[1], 0)


def kernel(
    nz, ny, plan,
    w_ref, qw, qm, qn, pw, pm, pn,
    out_ref,
    gw, gm, gn, vw, vm, vn, wide, part, got, tile, mixed, wide_stat, wide_all, mn_all,
    load_sem, pass_sem, send_sem, recv_sem, cross_sem, stat_sem,
):
    nc = nz * ny
    me = lax.axis_index("corpus")
    core = lax.axis_index("retrieve")
    other = 1 - core
    z, y = me // ny, me % ny
    rows = qw.shape[1]
    nq = rows * nc
    half = nq // 2
    nb = half // HALF
    slab = float(pw.shape[1] * nc)
    cols = pw.shape[1]
    own = (qw.at[0], qm, qn)
    full = (gw, gm, gn)
    held = (vw, vm, vn)
    source = (pw.at[0], pm, pn)

    barrier = pltpu.get_barrier_semaphore()

    up, down = z + 1 < nz, z > 0
    neighbours = 1 + (ny - 1) + up.astype(jnp.int32) + down.astype(jnp.int32)

    def greet(s):
        pl.semaphore_signal(barrier, inc=1, device_id={"corpus": s}, device_id_type=MESH)

    pl.semaphore_signal(barrier, inc=1, device_id={"retrieve": other}, device_id_type=MESH)
    each(ny - 1, lambda j: greet(z * ny + lax.rem(y + j + 1, ny)))
    pl.when(up)(lambda: greet(me + ny))
    pl.when(down)(lambda: greet(me - ny))

    def load(i):
        return pltpu.make_async_copy(
            own[i], full[i].at[pl.ds(pl.multiple_of(me * rows, rows), rows)], load_sem.at[i]
        )

    def load_pass(k):
        which, at, step = plan[k]
        return pltpu.make_async_copy(
            source[which].at[:, pl.ds(at, step)],
            held[which].at[:, pl.ds(at, step)],
            pass_sem.at[k],
        )

    for i in range(3):
        load(i).start()
    for k in range(sum(which > 0 for which, _, _ in plan)):
        load_pass(k).start()

    for i in range(3):
        load(i).wait()
    pl.semaphore_wait(barrier, neighbours)

    def block(k, s):
        which, at, step = plan[k]
        return full[which].at[pl.ds(pl.multiple_of(s * rows, rows), rows), pl.ds(at, step)]

    def push(k, s, to, way, src=None):
        which, at, step = plan[k]
        return pltpu.make_async_remote_copy(
            src_ref=block(k, s) if src is None else src,
            dst_ref=block(k, s),
            send_sem=send_sem.at[way, which],
            recv_sem=recv_sem.at[k, s],
            device_id={"corpus": to},
            device_id_type=MESH,
        )

    def first(k):
        which, at, step = plan[k]
        mine = None

        pl.when(up)(lambda: push(k, me, me + ny, 0, mine).start())
        pl.when(down)(lambda: push(k, me, me - ny, 1, mine).start())
        each(ny - 1, lambda j: push(k, me, z * ny + lax.rem(y + j + 1, ny), 2, mine).start())


    def relay(k, t):
        def arrived(s, more, ahead, way):
            push(k, s, me, way).wait_recv()
            pl.when(more)(lambda: push(k, s, ahead, way).start())
            each(ny - 1, lambda j: push(k, s, z * ny + lax.rem(y + j + 1, ny), 2).start())

        pl.when(z >= t)(lambda: arrived(me - t * ny, up, me + ny, 0))
        pl.when(z + t < nz)(lambda: arrived(me + t * ny, down, me - ny, 1))

    def collect(k):
        def column(i):
            def row(j):
                s = lax.rem(z + j, nz) * ny + lax.rem(y + i + 1, ny)
                push(k, s, me, 2).wait_recv()

            each(nz, row)

        each(ny - 1, column)

    def multiply(k):
        which, at, step = plan[k]
        load_pass(k).wait()
        into = (wide, part.at[0], part.at[1])[which]

        def product(t, r):
            n0 = pl.ds(pl.multiple_of(t * TILE, TILE), TILE)
            r0 = pl.ds(pl.multiple_of(r * LANES, LANES), LANES)
            value = lax.dot_general(
                full[which][r0, pl.ds(at, step)],
                held[which][n0, pl.ds(at, step)],
                (((1,), (1,)), ((), ())),
                preferred_element_type=jnp.float32,
            )
            if at == 0:
                into[r0, n0] = value
            else:
                into[r0, n0] += value

        each(nq // LANES, lambda r: each(cols // TILE, lambda t: product(t, r)))

    def cross(src, dst, i):
        return pltpu.make_async_remote_copy(
            src_ref=src,
            dst_ref=dst,
            send_sem=cross_sem.at[0, i],
            recv_sem=cross_sem.at[1, i],
            device_id={"retrieve": other},
            device_id_type=MESH,
        )

    def their_rows():
        return pl.ds(pl.multiple_of(other * half, half), half)

    def cross_part(i):
        return cross(part.at[i, their_rows()], got.at[i], i)

    def cross_tile():
        return cross(wide.at[their_rows()], tile, 2)

    def packed(peak, total):
        column = jnp.concatenate([peak, total], axis=0)
        return jnp.broadcast_to(column, (LANES, LANES)).T[0:1]

    def powers(score):
        peak = jnp.max(score, axis=1, keepdims=True)
        power = jnp.exp(score - peak)
        return power, packed(peak, jnp.sum(power, axis=1, keepdims=True))

    def factors(stats, mine, weight):
        top = jnp.max(stats, axis=0)
        grown = jnp.exp(stats - top[None])
        totals = jnp.stack([pltpu.roll(stats[s], HALF, 1) for s in range(stats.shape[0])])
        total = jnp.sum(grown * totals, axis=0)
        factor = jnp.exp(mine - top) * (slab / total) * weight
        return jnp.broadcast_to(factor, (LANES, LANES)).T[:HALF]

    def scaled(power, factor):
        return power * jnp.concatenate([factor] * (cols // LANES), axis=1)

    uniting = [w_ref[i].astype(jnp.float32) * (1.0 / 16.0) for i in range(4)]

    def mn_copy(to):
        return pltpu.make_async_remote_copy(
            src_ref=mn_all.at[me],
            dst_ref=mn_all.at[me],
            send_sem=stat_sem.at[0],
            recv_sem=stat_sem.at[1],
            device_id={"corpus": to},
            device_id_type=MESH,
        )

    def middle_stats():
        for i, width in ((0, MID), (1, NARROW)):
            cross_part(i).wait()
            for b in range(nb):
                rb = pl.ds(pl.multiple_of(core * half + b * HALF, HALF), HALF)
                gb = pl.ds(b * HALF, HALF)
                power, stat = powers((part[i, rb] + got[i, gb]) * (1.0 / math.sqrt(width)))
                got[i, gb] = power
                mn_all[me, i * nb + b] = stat
        each(nc - 1, lambda j: mn_copy(lax.rem(me + j + 1, nc)).start())

    def middle_mix():
        pltpu.make_async_remote_copy(
            src_ref=mn_all.at[pl.ds(0, nc - 1)],
            dst_ref=mn_all.at[pl.ds(0, nc - 1)],
            send_sem=stat_sem.at[0],
            recv_sem=stat_sem.at[1],
            device_id={"corpus": me},
            device_id_type=MESH,
        ).wait()
        for b in range(nb):
            gb = pl.ds(b * HALF, HALF)
            total = None
            for i in range(2):
                at = i * nb + b
                factor = factors(mn_all[:, at], mn_all[me, at], uniting[2 + i])
                term = scaled(got[i, gb], factor)
                total = term if total is None else total + term
            mixed[gb] = total

    def wide_copy(s, c):
        return pltpu.make_async_remote_copy(
            src_ref=wide_stat.at[c],
            dst_ref=wide_all.at[core * nc + me],
            send_sem=stat_sem.at[2],
            recv_sem=stat_sem.at[3],
            device_id={"corpus": s, "retrieve": c},
            device_id_type=MESH,
        )

    def wide_stats():
        for h in range(2):
            for b in range(nb):
                rb = pl.ds(h * half + b * HALF, HALF)
                power, stat = powers(wide[rb] * (1.0 / math.sqrt(WIDE)))
                wide[rb] = power
                wide_stat[h, b] = stat
        wide_all[core * nc + me] = wide_stat[core]

        def tell(j):
            s = lax.rem(me + j + 1, nc)
            for c in range(2):
                wide_copy(s, c).start()

        each(nc - 1, tell)
        wide_copy(me, other).start()
        cross_tile().start()

    def wide_mix():
        pltpu.make_async_remote_copy(
            src_ref=wide_all.at[pl.ds(0, 2 * nc - 1)],
            dst_ref=wide_all.at[pl.ds(0, 2 * nc - 1)],
            send_sem=stat_sem.at[2],
            recv_sem=stat_sem.at[3],
            device_id={"corpus": me},
            device_id_type=MESH,
        ).wait()
        here = [jnp.where(core == 0, uniting[0], uniting[1]), jnp.where(core == 0, uniting[1], uniting[0])]
        spans = []
        for b in range(nb):
            gb = pl.ds(b * HALF, HALF)
            rb = pl.ds(pl.multiple_of(core * half + b * HALF, HALF), HALF)
            mine = factors(wide_all[pl.ds(core * nc, nc), b], wide_all[core * nc + me, b], here[0])
            theirs = factors(wide_all[pl.ds(other * nc, nc), b], wide_all[other * nc + me, b], here[1])
            mixed[gb] += scaled(wide[rb], mine)
            spans.append((gb, theirs))
        cross_tile().wait()
        for gb, theirs in spans:
            out_ref[gb] = mixed[gb] + scaled(tile[gb], theirs)

    narrow_end = max(k for k in range(len(plan)) if plan[k][0] == 2)
    mid_end = max(k for k in range(len(plan)) if plan[k][0] == 1)
    early = range(mid_end + 1)
    late = range(mid_end + 1, len(plan))
    cut = mid_end + 1 + len(late) // 2
    for k in range(cut):
        first(k)
    for k in early:
        relay(k, 1)
    for k in range(cut, len(plan)):
        first(k)
    for t in range(2, nz):
        for k in early:
            relay(k, t)
    for t in range(1, nz):
        for k in late:
            relay(k, t)
            if t == 1:
                load_pass(k).start()
        if t == 1:
            for k in early:
                collect(k)
                multiply(k)
                if k == narrow_end:
                    cross_part(1).start()
            cross_part(0).start()
        if t == 2:
            middle_stats()
    for k in late:
        collect(k)
        multiply(k)
    wide_stats()
    middle_mix()
    wide_mix()

    def sent(way, i, count):
        some = full[i].at[pl.ds(0, count * rows)]
        pltpu.make_async_remote_copy(
            src_ref=some,
            dst_ref=some,
            send_sem=send_sem.at[way, i],
            recv_sem=recv_sem.at[0, 0],
            device_id={"corpus": me},
            device_id_type=MESH,
        ).wait_send()

    for i in range(3):
        for at in range(nz - 1):
            pl.when(z == at)(lambda i=i, at=at: sent(0, i, at + 1))
            pl.when(z == at + 1)(lambda i=i, at=at: sent(1, i, nz - at - 1))
        sent(2, i, nz * (ny - 1))


def body(weights, q_wide, q_mid, q_narrow, pass_wide, pass_mid, pass_narrow):
    nc = lax.axis_size("corpus")
    ny = 1
    while 4 * ny * ny <= nc:
        ny *= 2
    nz = nc // ny
    nq = q_wide.shape[1] * nc
    half = nq // 2
    nb = half // HALF
    cols = pass_wide.shape[1]
    wide_cols, mid_cols, narrow_cols = q_wide.shape[2], q_mid.shape[1], q_narrow.shape[1]
    plan = pieces(narrow_cols, mid_cols, wide_cols)
    f32, bf16 = jnp.float32, jnp.bfloat16
    hbm = pl.BlockSpec(memory_space=pl.ANY)
    features = wide_cols + mid_cols + narrow_cols
    return pl.pallas_call(
        functools.partial(kernel, nz, ny, plan),
        out_shape=jax.ShapeDtypeStruct((half, cols), f32),
        in_specs=[pl.BlockSpec(memory_space=pltpu.SMEM)] + [hbm] * 6,
        out_specs=pl.BlockSpec(memory_space=pltpu.VMEM),
        scratch_shapes=[
            pltpu.VMEM((nq, wide_cols), bf16),
            pltpu.VMEM((nq, mid_cols), bf16),
            pltpu.VMEM((nq, narrow_cols), bf16),
            pltpu.VMEM((cols, wide_cols), bf16),
            pltpu.VMEM((cols, mid_cols), bf16),
            pltpu.VMEM((cols, narrow_cols), bf16),
            pltpu.VMEM((nq, cols), f32),
            pltpu.VMEM((2, nq, cols), f32),
            pltpu.VMEM((2, half, cols), f32),
            pltpu.VMEM((half, cols), f32),
            pltpu.VMEM((half, cols), f32),
            pltpu.VMEM((2, nb, 1, LANES), f32),
            pltpu.VMEM((2 * nc, nb, 1, LANES), f32),
            pltpu.VMEM((nc, 2 * nb, 1, LANES), f32),
            pltpu.SemaphoreType.DMA((3,)),
            pltpu.SemaphoreType.DMA((len(plan),)),
            pltpu.SemaphoreType.DMA((3, 3)),
            pltpu.SemaphoreType.DMA((len(plan), nc)),
            pltpu.SemaphoreType.DMA((2, 3)),
            pltpu.SemaphoreType.DMA((4,)),
        ],
        compiler_params=pltpu.CompilerParams(
            collective_id=0, has_side_effects=True, vmem_limit_bytes=60 * 1024 * 1024
        ),
        cost_estimate=pl.CostEstimate(
            flops=2 * nq * cols * features,
            bytes_accessed=2 * cols * features,
            transcendentals=2 * nq * cols,
        ),
    )(weights, q_wide, q_mid, q_narrow, pass_wide, pass_mid, pass_narrow)


def solution(mesh):
    return jax.shard_map(
        body,
        mesh=mesh,
        in_specs=(
            P(),
            P("retrieve", ("groups", "corpus"), None),
            P(("groups", "corpus"), "retrieve"),
            P(("groups", "corpus"), "retrieve"),
            P("retrieve", ("groups", "corpus"), None),
            P(("groups", "corpus"), "retrieve"),
            P(("groups", "corpus"), "retrieve"),
        ),
        out_specs=P("retrieve", ("groups", "corpus")),
        check_vma=False,
    )
```
